256 devices in a mesh: dom: 64 (over z, y, core), sub: 4 (over x).
Axes of the slice: x: 4, y: 4, z: 8, core: 2. Of those that a mesh axis runs over, the one named last changes fastest.
Arguments:
- adjoint_start: float32 [512, 384], P(('dom', 'sub')), may hold values from -6 to 6
- source: float32 [512, 384], P(('dom', 'sub')), may hold values from -6 to 6
- jac_off: bfloat16 [512, 5, 384, 384], P(('dom', 'sub')), may hold values from -0.125 to 0.125
- jac_diag: bfloat16 [512, 384, 384], P(('dom', 'sub')), may hold values from -0.11 to 3.11
- precond: bfloat16 [512, 384, 384], P(('dom', 'sub')), may hold values from -1 to 1
- surf_map: bfloat16 [384, 384], replicated, may hold values from -0.3125 to 0.3125
- neighbours: int32 [512, 5], P(('dom', 'sub')), may hold values from 0 to 511, as said below
- owner: int32 [512], P(('dom', 'sub')), may hold values from 0 to 255
- surface_grad: float32 [256, 384], P(('dom', 'sub')), may hold values from -6 to 6
Outputs:
- adjoint: float32 [512, 384], P(('dom', 'sub'))
- sensitivity: float32 [256, 384], P(('dom', 'sub'))
The draws below stay inside these ranges and needn't reach their ends.
Inputs may be any that keep to these rules, and one draw needn't show every extreme that they name: `neighbours`: every device holds 2 consecutive block rows, devices taken dom-major. Slot 0 names a row of the same device; slots 1 and 2 name rows of the device one step higher and one step lower along dom, cyclically, with the same sub index; slots 3 and 4 likewise along sub.
All inputs are finite; a program needn't handle non-finite values.
Results may differ from the reference program's by a relative error of at most 0.0077.
Values may be sent and summed in bfloat16 or wider, within the bound.
No kernel may reach another device: no remote copies, remote signals or barrier semaphores. Data moves between devices by JAX's collectives and lax.ppermute only.
A program may use at most 64 MiB of HBM per device.

```python
import math
import jax
import jax.numpy as jnp
import numpy as np
from jax import lax

B = 384
S = 384
NEIGHBOURS = 5
ITERS = 2
ROWS_DEV = 2
DOMS = 64
SUBS = 4
BLOCKS = 512
PATCHES = 256


def dominant_blocks(key, lower, upper, noise, bound):
    key_diag, key_noise = jax.random.split(key)
    identity = (jnp.arange(B)[:, None] == jnp.arange(B)[None, :]).astype(jnp.float32)
    diagonal = jax.random.uniform(key_diag, (BLOCKS, 1, B), jnp.float32, lower, upper)
    spread = jnp.clip(jax.random.normal(key_noise, (BLOCKS, B, B), jnp.float32), -4.0, 4.0)
    scaled = jnp.clip(spread * (noise / math.sqrt(B)), -bound, bound)
    return (identity * diagonal + scaled).astype(jnp.bfloat16)


def draw_jac_diag(key, part):
    return dominant_blocks(jax.random.fold_in(key, 11), 1.5, 3.0, 0.5, 0.1)


def draw_precond(key, part):
    return dominant_blocks(jax.random.fold_in(key, 23), 0.3, 0.6, 0.1, 0.3)


def draw_neighbours(key, part):
    block_ids = jnp.arange(BLOCKS, dtype=jnp.int32)
    device_ids = block_ids // ROWS_DEV
    dom_index = device_ids // SUBS
    sub_index = device_ids % SUBS
    upper_dom = (dom_index + 1) % DOMS * SUBS + sub_index
    lower_dom = (dom_index + DOMS - 1) % DOMS * SUBS + sub_index
    upper_sub = dom_index * SUBS + (sub_index + 1) % SUBS
    lower_sub = dom_index * SUBS + (sub_index + SUBS - 1) % SUBS
    target_devices = jnp.stack([device_ids, upper_dom, lower_dom, upper_sub, lower_sub], axis=1)
    local_rows = jax.random.randint(jax.random.fold_in(key, 37), (BLOCKS, NEIGHBOURS), 0, ROWS_DEV, dtype=jnp.int32)
    return (target_devices * ROWS_DEV + local_rows).astype(jnp.int32)


def place_ends(result, key, least, largest):
    longest = result.shape.index(max(result.shape))
    spots = []
    for shift in (0, 1):
        where = [jax.random.randint(jax.random.fold_in(key, axis), (), 0, length) for axis, length in enumerate(result.shape)]
        where[longest] = (where[longest] + shift) % result.shape[longest]
        spots.append(tuple(where))
    return result.at[spots[0]].set(least).at[spots[1]].set(largest)


def block_scale(rng, extent, cuts, least, largest):
    def one(position, blocks):
        heights = jax.random.uniform(jax.random.fold_in(jax.random.fold_in(rng, 6), position), (blocks,), jnp.float32, least / len(cuts), largest / len(cuts))
        return jnp.repeat(jnp.exp(heights), extent[position] // blocks).reshape((-1,) + (1,) * (len(extent) - position - 1))

    loudness = one(*cuts[0])
    for cut in cuts[1:]:
        loudness = loudness * one(*cut)
    return loudness


def cumulative_ranks(amount, lean):
    portions = [(1 << 20) // math.isqrt(standing ** lean) + 1 for standing in range(1, amount + 1)]
    scale = 1 + sum(portions) // (1 << 30)
    return np.cumsum(np.array([max(1, weight // scale) for weight in portions]))


def ranked_ids(own_key, dims, number_of, lean):
    grid = cumulative_ranks(number_of, lean)
    lot = jax.random.randint(jax.random.fold_in(own_key, 1), dims, 0, int(grid[number_of - 1]))
    standing = jnp.searchsorted(jnp.asarray(grid, jnp.int32), lot, side="right")
    return jax.random.permutation(jax.random.fold_in(own_key, 2), number_of)[standing].astype(jnp.int32)


def gaussian(rng, extent, deviation, limit, cuts=(), held_as=jnp.bfloat16):
    values = jax.random.normal(rng, extent, jnp.float32) * deviation
    if len(cuts) > 0:
        values = block_scale(rng, extent, cuts, -0.22, 0.18) * values
    return jnp.clip(values, min=-limit, max=limit).astype(held_as)


def setup_inputs(seed: int = 0) -> dict:
    arg_keys = jax.random.split(jax.random.key(seed), 10)
    return {
        "adjoint_start": gaussian(arg_keys[0], (BLOCKS, B), 1.0, 6.0, ((0, 256),), jnp.float32),
        "source": gaussian(arg_keys[1], (BLOCKS, B), 1.0, 6.0, ((0, 256),), jnp.float32),
        "jac_off": gaussian(arg_keys[2], (BLOCKS, NEIGHBOURS, B, B), (5 * B) ** -0.5, 0.125, ((0, 256),)),
        "jac_diag": draw_jac_diag(jax.random.fold_in(arg_keys[9], 71), 0),
        "precond": draw_precond(jax.random.fold_in(arg_keys[9], 71), 0),
        "surf_map": gaussian(arg_keys[5], (B, S), B ** -0.5, 0.3125),
        "neighbours": draw_neighbours(jax.random.fold_in(arg_keys[9], 71), 0),
        "owner": place_ends(ranked_ids(arg_keys[7], (BLOCKS,), PATCHES, 2), jax.random.fold_in(arg_keys[7], 3), 0, PATCHES - 1).astype(jnp.int32),
        "surface_grad": gaussian(arg_keys[8], (PATCHES, S), 1.0, 6.0, ((0, 256),), jnp.float32),
    }


def row_terms(items):
    low_row, off_row, diag_row = items
    partials = jnp.einsum("b,kbc->kc", low_row.astype(jnp.float32), off_row.astype(jnp.float32))
    own_term = jnp.einsum("b,bc->c", low_row.astype(jnp.float32), diag_row.astype(jnp.float32))
    return partials, own_term


def apply_precond(items):
    resid_row, precond_row = items
    return jnp.einsum("b,bc->c", resid_row.astype(jnp.float32), precond_row.astype(jnp.float32))


def reference(adjoint_start, source, jac_off, jac_diag, precond, surf_map, neighbours, owner, surface_grad):
    adjoint = adjoint_start
    flat_targets = neighbours.reshape(-1).astype(jnp.int32)
    for iteration in range(ITERS):
        adjoint_low = adjoint.astype(jnp.bfloat16)
        partials, own_term = lax.map(row_terms, (adjoint_low, jac_off, jac_diag))
        pushed = jnp.zeros((BLOCKS, B), jnp.float32).at[flat_targets].add(partials.reshape(-1, B))
        transposed = own_term + pushed
        residual = source - transposed
        residual_low = residual.astype(jnp.bfloat16)
        adjoint = adjoint + lax.map(apply_precond, (residual_low, precond))
    final_low = adjoint.astype(jnp.bfloat16)
    contribution = jnp.dot(final_low, surf_map, preferred_element_type=jnp.float32).astype(jnp.bfloat16)
    summed = jnp.zeros((PATCHES, S), jnp.float32).at[owner.astype(jnp.int32)].add(contribution.astype(jnp.float32))
    sensitivity = surface_grad - summed
    return adjoint, sensitivity
```

```python
import jax
import jax.numpy as jnp
from jax import lax
from jax.sharding import Mesh, PartitionSpec as P

ITERS = 2
CUT = {"z": 8, "y": 4, "core": 2, "x": 4}
ALL = tuple(CUT)


def pairs(axis, first):
    subs = CUT["x"]
    devices = CUT["z"] * CUT["y"] * CUT["core"] * subs
    route = []
    for device in range(devices):
        dom, sub = divmod(device, subs)
        if axis == "dom":
            doms = devices // subs
            dom = (((dom - first) % doms ^ 1) + first) % doms
        else:
            sub = (((sub - first) % subs ^ 1) + first) % subs
        route.append((device, dom * subs + sub))
    return route


def collect(partials, rows, column):
    matches = rows[:, column][:, None] == jnp.arange(partials.shape[0], dtype=jnp.int32)[None, :]
    spread = jnp.where(matches[:, :, None], partials[:, column][:, None, :], jnp.float32(0.0))
    return jnp.sum(spread, axis=0)


def on_device(
    adjoint_start, source, jac_off, jac_diag, precond, surf_map, neighbours, owner, surface_grad
):
    row_count, width = adjoint_start.shape
    rows = neighbours % row_count
    even_dom = lax.axis_index("core") == 0
    even_sub = lax.axis_index("x") % 2 == 0
    adjoint = adjoint_start
    for _ in range(ITERS):
        adjoint_low = adjoint.astype(jnp.bfloat16)
        partials = jnp.einsum(
            "rb,rkbc->rkc", adjoint_low, jac_off, preferred_element_type=jnp.float32
        )
        up_dom, down_dom, up_sub, down_sub = (collect(partials, rows, k) for k in range(1, 5))
        came = [
            lax.ppermute(jnp.where(even_dom, up_dom, down_dom), ALL, pairs("dom", 0)),
            lax.ppermute(jnp.where(even_sub, up_sub, down_sub), ALL, pairs("sub", 0)),
            lax.ppermute(jnp.where(even_sub, down_sub, up_sub), ALL, pairs("sub", 1)),
            lax.ppermute(jnp.where(even_dom, down_dom, up_dom), ALL, pairs("dom", 1)),
        ]
        own_term = jnp.einsum(
            "rb,rbc->rc", adjoint_low, jac_diag, preferred_element_type=jnp.float32
        )
        transposed = own_term + collect(partials, rows, 0)
        for part in came:
            transposed = transposed + part
        residual_low = (source - transposed).astype(jnp.bfloat16)
        adjoint = adjoint + jnp.einsum(
            "rb,rbc->rc", residual_low, precond, preferred_element_type=jnp.float32
        )
    final_low = adjoint.astype(jnp.bfloat16)
    contribution = jnp.dot(final_low, surf_map, preferred_element_type=jnp.float32).astype(
        jnp.bfloat16
    )
    plane = CUT["y"] * CUT["x"]
    tagged = jnp.concatenate(
        [contribution, jnp.broadcast_to(owner.astype(jnp.bfloat16)[:, None], (row_count, 128))],
        axis=1,
    )
    got = lax.all_to_all(
        jnp.broadcast_to(tagged[None], (plane, row_count, width + 128)),
        ("y", "x"), 0, 0, tiled=True,
    ).reshape(plane * row_count, width + 128)
    owners = got[:, width].astype(jnp.int32)
    line = CUT["z"] * CUT["core"]
    place = jnp.arange(line, dtype=jnp.int32)
    z, core = place // CUT["core"], place % CUT["core"]
    patch = ((z * CUT["y"] + lax.axis_index("y")) * CUT["core"] + core) * CUT["x"] + lax.axis_index("x")
    onehot = (patch[:, None] == owners[None, :]).astype(jnp.bfloat16)
    sums = jnp.dot(onehot, got[:, :width], preferred_element_type=jnp.float32)
    parts = lax.all_to_all(sums, ("z", "core"), 0, 0, tiled=True)
    sensitivity = surface_grad - jnp.sum(parts, axis=0, keepdims=True)
    return (adjoint, sensitivity)


def solution(mesh):
    cut = Mesh(mesh.devices.reshape(tuple(CUT.values())), ALL)
    return jax.shard_map(
        on_device,
        mesh=cut,
        in_specs=(
            P(ALL, None),
            P(ALL, None),
            P(ALL, None, None, None),
            P(ALL, None, None),
            P(ALL, None, None),
            P(),
            P(ALL, None),
            P(ALL),
            P(ALL, None),
        ),
        out_specs=(P(ALL, None), P(ALL, None)),
        check_vma=False,
    )
```

```python
import jax
import jax.numpy as jnp
from jax import lax
from jax.experimental import pallas as pl
from jax.experimental.pallas import tpu as pltpu
from jax.sharding import Mesh, PartitionSpec as P

CUT = {"z": 8, "y": 4, "core": 2, "x": 4}
ALL = tuple(CUT)
LANES = 128
F32 = jnp.float32
BF16 = jnp.bfloat16
VMEM = pl.BlockSpec(memory_space=pltpu.VMEM)
SMEM = pl.BlockSpec(memory_space=pltpu.SMEM)
HBM = pl.BlockSpec(memory_space=pltpu.HBM)


def pairs(axis, first):
    subs = CUT["x"]
    devices = CUT["z"] * CUT["y"] * CUT["core"] * subs
    route = []
    for device in range(devices):
        dom, sub = divmod(device, subs)
        if axis == "dom":
            doms = devices // subs
            dom = (((dom - first) % doms ^ 1) + first) % doms
        else:
            sub = (((sub - first) % subs ^ 1) + first) % subs
        route.append((device, dom * subs + sub))
    return route


def placed(values, row, target):
    rows = lax.broadcasted_iota(jnp.int32, (8, values.shape[1]), 0)
    return jnp.where(rows == target, values[row : row + 1, :], 0.0).astype(BF16)


def matmul(left, right):
    return jnp.dot(left, right, preferred_element_type=F32)


def message_slots():
    core, odd = lax.axis_index("core"), lax.axis_index("x") % 2
    return 1 + core, 3 + odd, 4 - odd, 2 - core


def message(values, names_ref, slot, off_ref):
    count = values.shape[0]
    total = None
    for row in range(count):
        part = matmul(placed(values, row, names_ref[row, slot] % count), off_ref[row])
        total = part if total is None else total + part
    return total[:count]


def step(adjoint, source, local, came, precond_ref):
    residual = source - local
    for part in came:
        residual = residual - part[...]
    for row in range(adjoint.shape[0]):
        adjoint = adjoint + matmul(placed(residual, row, row), precond_ref[row])[: adjoint.shape[0]]
    return adjoint


def first_kernel(names_in, adjoint_in, off_in, c0, c1, c2, c3, names, adjoint, off, sems):
    slots = message_slots()
    copies = [
        pltpu.make_async_copy(off_in.at[:, slot], off.at[m], sems.at[m])
        for m, slot in enumerate(slots)
    ]
    heads = [
        pltpu.make_async_copy(names_in, names, sems.at[len(slots)]),
        pltpu.make_async_copy(adjoint_in, adjoint, sems.at[len(slots) + 1]),
    ]
    for copy in heads + copies:
        copy.start()
    for copy in heads:
        copy.wait()
    for m, (slot, out) in enumerate(zip(slots, (c0, c1, c2, c3), strict=True)):
        copies[m].wait()
        out[...] = message(adjoint[...], names, slot, off.at[m])


def local_kernel(names, adjoint, off, diag, out):
    values = adjoint[...]
    count = values.shape[0]
    total = None
    for row in range(values.shape[0]):
        part = matmul(placed(values, row, names[row, 0] % count), off[row, 0])
        part = part + matmul(placed(values, row, row), diag[row])
        total = part if total is None else total + part
    out[...] = total[: values.shape[0]]


def middle_kernel(names, adjoint, source, local, c0, c1, c2, c3, precond, off, new, *outs):
    values = step(adjoint[...], source[...], local[...], (c0, c1, c2, c3), precond)
    new[...] = values
    for slot, out in zip(message_slots(), outs, strict=True):
        out[...] = message(values, names, slot, off.at[:, slot])


def last_kernel(owner, adjoint, source, local, c0, c1, c2, c3, precond, surf, new, payload):
    values = step(adjoint[...], source[...], local[...], (c0, c1, c2, c3), precond)
    new[...] = values
    count, width = values.shape
    left = sum(placed(values, row, row) for row in range(count))
    contribution = matmul(left, surf[...]).astype(BF16).astype(F32)
    lanes = width // LANES
    tile = [
        contribution[row : row + 1, i * LANES : (i + 1) * LANES]
        for row in range(count)
        for i in range(lanes)
    ]
    tile += [jnp.full((1, LANES), owner[row].astype(F32)) for row in range(count)]
    tile = jnp.concatenate(tile, axis=0)
    for i in range(payload.shape[0]):
        payload[i] = tile


def spread_kernel(got, out):
    peers = got.shape[0]
    lanes = (got.shape[1] - 2) // 2
    lane = lax.broadcasted_iota(jnp.int32, (peers, LANES), 1)
    patch = (lane // CUT["core"]) * (CUT["y"] * CUT["core"] * CUT["x"])
    patch = patch + (lane % CUT["core"]) * CUT["x"]
    patch = patch + lax.axis_index("y") * (CUT["core"] * CUT["x"]) + lax.axis_index("x")
    line = out.shape[0]
    patch = jnp.where(lane < line, patch, -1).astype(F32)
    hot = jnp.concatenate(
        [jnp.where(got[:, 2 * lanes + row, :] == patch, 1.0, 0.0).astype(BF16) for row in range(2)],
        axis=0,
    )
    for i in range(lanes):
        rows = jnp.concatenate([got[:, i, :], got[:, lanes + i, :]], axis=0).astype(BF16)
        sums = lax.dot_general(hot, rows, (((0,), (0,)), ((), ())), preferred_element_type=F32)
        out[:, i, :] = sums[:line]
    for i in range(lanes, out.shape[1]):
        out[:, i, :] = jnp.zeros((line, LANES), F32)


def finish_kernel(grad, parts, out):
    total = jnp.sum(parts[...], axis=0)
    for i in range(grad.shape[1] // LANES):
        where = slice(i * LANES, (i + 1) * LANES)
        out[:, where] = grad[:, where] - total[i : i + 1, :]


def call(kernel, specs, outs, name, flops=0, nbytes=0, scratch=(), vmem=8):
    return pl.pallas_call(
        kernel,
        in_specs=specs,
        out_specs=[VMEM] * len(outs),
        out_shape=outs,
        scratch_shapes=scratch,
        name=name,
        compiler_params=pltpu.CompilerParams(vmem_limit_bytes=vmem << 20),
        cost_estimate=pl.CostEstimate(flops=flops, bytes_accessed=nbytes, transcendentals=0),
    )


def on_device(
    adjoint_start, source, jac_off, jac_diag, precond, surf_map, neighbours, owner, surface_grad
):
    count, width = adjoint_start.shape
    routes = [pairs("dom", 0), pairs("sub", 0), pairs("sub", 1), pairs("dom", 1)]
    block = jax.ShapeDtypeStruct((count, width), F32)

    def swap(messages):
        return [lax.ppermute(m, ALL, route) for m, route in zip(messages, routes, strict=True)]

    matrix = width * width
    messages = call(
        first_kernel,
        [HBM] * 3,
        [block] * 4,
        "first",
        16 * matrix,
        16 * matrix,
        [
            pltpu.SMEM(neighbours.shape, jnp.int32),
            pltpu.VMEM((count, width), F32),
            pltpu.VMEM((4, count, width, width), BF16),
            pltpu.SemaphoreType.DMA((6,)),
        ],
        vmem=63,
    )(neighbours, adjoint_start, jac_off)
    came = swap(messages)
    local_call = call(
        local_kernel, [SMEM, VMEM, VMEM, VMEM], [block], "local", 8 * matrix, 8 * matrix
    )
    (local,) = local_call(neighbours, adjoint_start, jac_off, jac_diag)
    adjoint, *messages = call(
        middle_kernel, [SMEM] + [VMEM] * 9, [block] * 5, "middle", 20 * matrix, 20 * matrix
    )(neighbours, adjoint_start, source, local, *came, precond, jac_off)
    came = swap(messages)
    (local,) = local_call(neighbours, adjoint, jac_off, jac_diag)

    plane = CUT["y"] * CUT["x"]
    line = CUT["z"] * CUT["core"]
    adjoint, payload = call(
        last_kernel,
        [SMEM] + [VMEM] * 9,
        [block, jax.ShapeDtypeStruct((plane, 8, LANES), F32)],
        "last",
        6 * matrix,
        6 * matrix,
    )(owner, adjoint, source, local, *came, precond, surf_map)
    got = lax.all_to_all(payload, ("y", "x"), 0, 0, tiled=True)
    (sums,) = call(
        spread_kernel, [VMEM], [jax.ShapeDtypeStruct((line, 8, LANES), F32)], "spread"
    )(got)
    parts = lax.all_to_all(sums, ("z", "core"), 0, 0, tiled=True)
    (sensitivity,) = call(
        finish_kernel, [VMEM, VMEM], [jax.ShapeDtypeStruct((1, width), F32)], "finish"
    )(surface_grad, parts)
    return (adjoint, sensitivity)


def solution(mesh):
    cut = Mesh(mesh.devices.reshape(tuple(CUT.values())), ALL)
    return jax.shard_map(
        on_device,
        mesh=cut,
        in_specs=(
            P(ALL, None),
            P(ALL, None),
            P(ALL, None, None, None),
            P(ALL, None, None),
            P(ALL, None, None),
            P(),
            P(ALL, None),
            P(ALL),
            P(ALL, None),
        ),
        out_specs=(P(ALL, None), P(ALL, None)),
        check_vma=False,
    )
```

```python
import math

import jax
import jax.numpy as jnp
from jax import lax
from jax.experimental import pallas as pl
from jax.experimental.pallas import tpu as pltpu
from jax.sharding import Mesh, PartitionSpec as P

CUT = {"z": 8, "y": 4, "core": 2, "x": 4}
ALL = tuple(CUT)
LANES = 128
FIRST, SECOND = ('z', 'core'), ('y', 'x')
ORDER = (3, 1, 2, 0)
F32 = jnp.float32
BF16 = jnp.bfloat16
VMEM = pl.BlockSpec(memory_space=pltpu.VMEM)
HBM = pl.BlockSpec(memory_space=pltpu.HBM)


def pairs(axis, first):
    subs = CUT["x"]
    devices = CUT["z"] * CUT["y"] * CUT["core"] * subs
    route = []
    for device in range(devices):
        dom, sub = divmod(device, subs)
        if axis == "dom":
            doms = devices // subs
            dom = (((dom - first) % doms ^ 1) + first) % doms
        else:
            sub = (((sub - first) % subs ^ 1) + first) % subs
        route.append((device, dom * subs + sub))
    return route


def placed(row, count, target):
    rows = lax.broadcasted_iota(jnp.int32, (count, row.shape[1]), 0)
    return jnp.where(rows == target, row, 0.0).astype(BF16)


def matmul(left, right):
    return jnp.dot(left, right, preferred_element_type=F32)


def message_slots():
    core, odd = lax.axis_index("core"), lax.axis_index("x") % 2
    four = (1, 2, core), (3, 4, odd), (4, 3, odd), (2, 1, core)
    return [four[i] for i in ORDER]


def step(adjoint, source, local, came, precond_ref):
    residual = source - local
    for part in came:
        residual = residual - part[...]
    count = adjoint.shape[0]
    for row in range(count):
        left = placed(residual[row : row + 1, :], count, row)
        adjoint = adjoint + matmul(left, precond_ref[row])
    return adjoint


def send_all(values, names, off, outs):
    count = values.shape[0]
    for (even, odd, which), out, blocks in zip(message_slots(), outs, off, strict=True):
        total = jnp.zeros(out.shape, F32)
        for row in range(count):
            here = slice(row, row + 1)
            name = jnp.where(which == 0, names[here, even : even + 1], names[here, odd : odd + 1])
            left = placed(values[here, :], count, name % count)
            total = total + matmul(left, blocks(row))
        out[...] = total


def first_kernel(names_in, adjoint_in, off_in, c0, c1, c2, c3, off, names, adjoint, sems):
    slots = [jnp.where(which == 0, even, odd) for even, odd, which in message_slots()]
    heads = [
        pltpu.make_async_copy(names_in, names, sems.at[5]),
        pltpu.make_async_copy(adjoint_in, adjoint, sems.at[6]),
    ]
    blocks = [
        pltpu.make_async_copy(off_in.at[:, slot], off.at[:, slot], sems.at[m])
        for m, slot in enumerate(slots + [0])
    ]
    for copy in heads + blocks:
        copy.start()
    for copy in heads:
        copy.wait()

    def arrived(m, slot):
        def block(row):
            if row == 0:
                blocks[m].wait()
            return off[row, slot]

        return block

    send_all(
        adjoint[...], names, [arrived(m, slot) for m, slot in enumerate(slots)], (c0, c1, c2, c3)
    )
    blocks[-1].wait()


def local_kernel(names, adjoint, off, diag, out):
    count = adjoint.shape[0]
    total = jnp.zeros(out.shape, F32)
    for row in range(count):
        values = adjoint[row : row + 1, :]
        total = total + matmul(placed(values, count, names[row : row + 1, 0:1] % count), off[row, 0])
        total = total + matmul(placed(values, count, row), diag[row])
    out[...] = total


def middle_kernel(names, adjoint, source, local, c0, c1, c2, c3, precond, off, new, *outs):
    values = step(adjoint[...], source[...], local[...], (c0, c1, c2, c3), precond)
    new[...] = values
    slots = [jnp.where(which == 0, even, odd) for even, odd, which in message_slots()]
    send_all(values, names, [lambda row, slot=slot: off[row, slot] for slot in slots], outs)


def last_kernel(owner, adjoint, source, local, c0, c1, c2, c3, precond, surf, new, payload):
    values = step(adjoint[...], source[...], local[...], (c0, c1, c2, c3), precond)
    new[...] = values
    count, width = values.shape
    contribution = matmul(values.astype(BF16), surf[...]).astype(BF16).astype(F32)
    tile = [
        contribution[row : row + 1, i * LANES : (i + 1) * LANES]
        for row in range(count)
        for i in range(width // LANES)
    ]
    tile += [
        jnp.broadcast_to(owner[0:1, row : row + 1].astype(F32), (1, LANES)) for row in range(count)
    ]
    tile = jnp.concatenate(tile, axis=0)
    for i in range(payload.shape[0]):
        payload[i] = tile


def stride(axis):
    step = 1
    for name in reversed(ALL):
        if name == axis:
            return step
        step *= CUT[name]
    raise ValueError(axis)


def spread_kernel(got, out):
    peers = got.shape[0]
    lanes = (got.shape[1] - 2) // 2
    lane = lax.broadcasted_iota(jnp.int32, (peers, LANES), 1)
    patch = sum(lax.axis_index(axis) * stride(axis) for axis in FIRST)
    place = lane
    for axis in reversed(SECOND):
        patch = patch + place % CUT[axis] * stride(axis)
        place = place // CUT[axis]
    group = out.shape[0]
    patch = jnp.where(lane < group, patch, -1).astype(F32)
    hot = jnp.concatenate(
        [jnp.where(got[:, 2 * lanes + row, :] == patch, 1.0, 0.0).astype(BF16) for row in range(2)],
        axis=0,
    )
    for i in range(lanes):
        rows = jnp.concatenate([got[:, i, :], got[:, lanes + i, :]], axis=0).astype(BF16)
        sums = lax.dot_general(hot, rows, (((0,), (0,)), ((), ())), preferred_element_type=F32)
        out[:, i, :] = sums[:group]
    for i in range(lanes, out.shape[1]):
        out[:, i, :] = jnp.zeros((group, LANES), F32)


def finish_kernel(grad, parts, out):
    total = jnp.sum(parts[...], axis=0)
    for i in range(grad.shape[1] // LANES):
        where = slice(i * LANES, (i + 1) * LANES)
        out[:, where] = grad[:, where] - total[i : i + 1, :]


def call(kernel, specs, outs, name, flops=0, nbytes=0, scratch=(), vmem=8):
    return pl.pallas_call(
        kernel,
        in_specs=specs,
        out_specs=[VMEM] * len(outs),
        out_shape=outs,
        scratch_shapes=scratch,
        name=name,
        compiler_params=pltpu.CompilerParams(vmem_limit_bytes=vmem << 20),
        cost_estimate=pl.CostEstimate(flops=flops, bytes_accessed=nbytes, transcendentals=0),
    )


def on_device(
    adjoint_start, source, jac_off, jac_diag, precond, surf_map, neighbours, owner, surface_grad
):
    count, width = adjoint_start.shape
    routes = [pairs("dom", 0), pairs("sub", 0), pairs("sub", 1), pairs("dom", 1)]
    routes = [routes[i] for i in ORDER]
    block = jax.ShapeDtypeStruct((count, width), F32)

    def swap(messages):
        return [lax.ppermute(m, ALL, route) for m, route in zip(messages, routes, strict=True)]

    matrix = width * width
    *messages, off = call(
        first_kernel,
        [HBM] * 3,
        [pltpu.VMEM((count, width), F32)] * 4 + [pltpu.VMEM(jac_off.shape, BF16)],
        "first",
        16 * matrix,
        16 * matrix,
        [
            pltpu.VMEM(neighbours.shape, jnp.int32),
            pltpu.VMEM((count, width), F32),
            pltpu.SemaphoreType.DMA((7,)),
        ],
        52,
    )(neighbours, adjoint_start, jac_off)
    came = swap(messages)
    local_call = call(local_kernel, [VMEM] * 4, [block], "local", 8 * matrix, 8 * matrix)
    (local,) = local_call(neighbours, adjoint_start, off, jac_diag)
    adjoint, *messages = call(
        middle_kernel, [VMEM] * 10, [block] * 5, "middle", 20 * matrix, 20 * matrix
    )(neighbours, adjoint_start, source, local, *came, precond, off)
    came = swap(messages)
    (local,) = local_call(neighbours, adjoint, off, jac_diag)

    plane = math.prod(CUT[axis] for axis in FIRST)
    line = math.prod(CUT[axis] for axis in SECOND)
    adjoint, payload = call(
        last_kernel,
        [VMEM] * 10,
        [block, jax.ShapeDtypeStruct((plane, 8, LANES), F32)],
        "last",
        6 * matrix,
        6 * matrix,
    )(owner.reshape(1, count), adjoint, source, local, *came, precond, surf_map)
    got = lax.all_to_all(payload, FIRST, 0, 0, tiled=True)
    (sums,) = call(
        spread_kernel, [VMEM], [jax.ShapeDtypeStruct((line, 8, LANES), F32)], "spread"
    )(got)
    parts = lax.all_to_all(sums, SECOND, 0, 0, tiled=True)
    (sensitivity,) = call(
        finish_kernel, [VMEM, VMEM], [jax.ShapeDtypeStruct((1, width), F32)], "finish"
    )(surface_grad, parts)
    return (adjoint, sensitivity)


def solution(mesh):
    cut = Mesh(mesh.devices.reshape(tuple(CUT.values())), ALL)
    return jax.shard_map(
        on_device,
        mesh=cut,
        in_specs=(
            P(ALL, None),
            P(ALL, None),
            P(ALL, None, None, None),
            P(ALL, None, None),
            P(ALL, None, None),
            P(),
            P(ALL, None),
            P(ALL),
            P(ALL, None),
        ),
        out_specs=(P(ALL, None), P(ALL, None)),
        check_vma=False,
    )
```

```python
import math

import jax
import jax.numpy as jnp
from jax import lax
from jax.experimental import pallas as pl
from jax.experimental.pallas import tpu as pltpu
from jax.sharding import Mesh, PartitionSpec as P

CUT = {"z": 8, "y": 4, "core": 2, "x": 4}
ALL = tuple(CUT)
LANES = 128
FIRST, SECOND = ('z', 'core'), ('y', 'x')
ORDER = (3, 1, 2, 0)
F32 = jnp.float32
BF16 = jnp.bfloat16
VMEM = pl.BlockSpec(memory_space=pltpu.VMEM)
HBM = pl.BlockSpec(memory_space=pltpu.HBM)


def pairs(axis, first):
    subs = CUT["x"]
    devices = CUT["z"] * CUT["y"] * CUT["core"] * subs
    route = []
    for device in range(devices):
        dom, sub = divmod(device, subs)
        if axis == "dom":
            doms = devices // subs
            dom = (((dom - first) % doms ^ 1) + first) % doms
        else:
            sub = (((sub - first) % subs ^ 1) + first) % subs
        route.append((device, dom * subs + sub))
    return route


def placed(row, count, target):
    rows = lax.broadcasted_iota(jnp.int32, (count, row.shape[1]), 0)
    return jnp.where(rows == target, row, 0.0).astype(BF16)


def matmul(left, right):
    return jnp.dot(left, right, preferred_element_type=F32)


def message_slots():
    core, odd = lax.axis_index("core"), lax.axis_index("x") % 2
    four = (1, 2, core), (3, 4, odd), (4, 3, odd), (2, 1, core)
    return [four[i] for i in ORDER]


def step(adjoint, source, local, came, precond_ref):
    residual = source - local
    for part in came:
        residual = residual - part[...]
    count = adjoint.shape[0]
    for row in range(count):
        left = placed(residual[row : row + 1, :], count, row)
        adjoint = adjoint + matmul(left, precond_ref[row])
    return adjoint


def send_all(values, names, off, outs):
    count = values.shape[0]
    for (even, odd, which), out, blocks in zip(message_slots(), outs, off, strict=True):
        total = jnp.zeros(out.shape, F32)
        for row in range(count):
            here = slice(row, row + 1)
            name = jnp.where(which == 0, names[here, even : even + 1], names[here, odd : odd + 1])
            left = placed(values[here, :], count, name % count)
            total = total + matmul(left, blocks(row))
        out[...] = total


def first_kernel(names_in, adjoint_in, off_in, c0, c1, c2, c3, off, names, adjoint, left, sums, sems):
    slots = [jnp.where(which == 0, even, odd) for even, odd, which in message_slots()]
    count = adjoint.shape[0]
    heads = [
        pltpu.make_async_copy(names_in, names, sems.at[5]),
        pltpu.make_async_copy(adjoint_in, adjoint, sems.at[6]),
    ]

    def block(m):
        slot = sum(jnp.where(m == i, slots[i], 0) for i in range(len(slots)))
        return slot, pltpu.make_async_copy(off_in.at[:, slot], off.at[:, slot], sems.at[m])

    for copy in heads:
        copy.start()

    @pl.loop(0, len(slots) + 1)
    def _(m):
        block(m)[1].start()

    for copy in heads:
        copy.wait()
    for m, (even, odd, which) in enumerate(message_slots()):
        for row in range(count):
            here = slice(row, row + 1)
            name = jnp.where(which == 0, names[here, even : even + 1], names[here, odd : odd + 1])
            left[m, row] = placed(adjoint[here, :], count, name % count)

    @pl.loop(0, len(slots))
    def _(m):
        slot, copy = block(m)
        copy.wait()
        sums[m] = jnp.zeros(sums.shape[1:], F32)

        @pl.loop(0, count)
        def _(row):
            sums[m] += matmul(left[m, row], off[row, slot])

    for m, out in enumerate((c0, c1, c2, c3)):
        out[...] = sums[m]
    block(len(slots))[1].wait()


def local_kernel(names, adjoint, off, diag, out):
    count = adjoint.shape[0]
    total = jnp.zeros(out.shape, F32)
    for row in range(count):
        values = adjoint[row : row + 1, :]
        total = total + matmul(placed(values, count, names[row : row + 1, 0:1] % count), off[row, 0])
        total = total + matmul(placed(values, count, row), diag[row])
    out[...] = total


def middle_kernel(names, adjoint, source, local, c0, c1, c2, c3, precond, off, new, *outs):
    values = step(adjoint[...], source[...], local[...], (c0, c1, c2, c3), precond)
    new[...] = values
    slots = [jnp.where(which == 0, even, odd) for even, odd, which in message_slots()]
    send_all(values, names, [lambda row, slot=slot: off[row, slot] for slot in slots], outs)


def last_kernel(owner, adjoint, source, local, c0, c1, c2, c3, precond, surf, new, payload):
    values = step(adjoint[...], source[...], local[...], (c0, c1, c2, c3), precond)
    new[...] = values
    count, width = values.shape
    contribution = matmul(values.astype(BF16), surf[...]).astype(BF16).astype(F32)
    tile = [
        contribution[row : row + 1, i * LANES : (i + 1) * LANES]
        for row in range(count)
        for i in range(width // LANES)
    ]
    tile += [
        jnp.broadcast_to(owner[0:1, row : row + 1].astype(F32), (1, LANES)) for row in range(count)
    ]
    tile = jnp.concatenate(tile, axis=0)
    for i in range(payload.shape[0]):
        payload[i] = tile


def stride(axis):
    step = 1
    for name in reversed(ALL):
        if name == axis:
            return step
        step *= CUT[name]
    raise ValueError(axis)


def spread_kernel(got, out):
    peers = got.shape[0]
    lanes = (got.shape[1] - 2) // 2
    lane = lax.broadcasted_iota(jnp.int32, (peers, LANES), 1)
    patch = sum(lax.axis_index(axis) * stride(axis) for axis in FIRST)
    place = lane
    for axis in reversed(SECOND):
        patch = patch + place % CUT[axis] * stride(axis)
        place = place // CUT[axis]
    group = out.shape[0]
    patch = jnp.where(lane < group, patch, -1).astype(F32)
    hot = jnp.concatenate(
        [jnp.where(got[:, 2 * lanes + row, :] == patch, 1.0, 0.0).astype(BF16) for row in range(2)],
        axis=0,
    )
    for i in range(lanes):
        rows = jnp.concatenate([got[:, i, :], got[:, lanes + i, :]], axis=0).astype(BF16)
        sums = lax.dot_general(hot, rows, (((0,), (0,)), ((), ())), preferred_element_type=F32)
        out[:, i, :] = sums[:group]
    for i in range(lanes, out.shape[1]):
        out[:, i, :] = jnp.zeros((group, LANES), F32)


def finish_kernel(grad, parts, values, adjoint, out):
    adjoint[...] = values[...]
    total = jnp.sum(parts[...], axis=0)
    for i in range(grad.shape[1] // LANES):
        where = slice(i * LANES, (i + 1) * LANES)
        out[:, where] = grad[:, where] - total[i : i + 1, :]


def call(kernel, specs, outs, name, flops=0, nbytes=0, scratch=(), vmem=8):
    return pl.pallas_call(
        kernel,
        in_specs=specs,
        out_specs=[VMEM] * len(outs),
        out_shape=outs,
        scratch_shapes=scratch,
        name=name,
        compiler_params=pltpu.CompilerParams(vmem_limit_bytes=vmem << 20),
        cost_estimate=pl.CostEstimate(flops=flops, bytes_accessed=nbytes, transcendentals=0),
    )


def on_device(
    adjoint_start, source, jac_off, jac_diag, precond, surf_map, neighbours, owner, surface_grad
):
    count, width = adjoint_start.shape
    routes = [pairs("dom", 0), pairs("sub", 0), pairs("sub", 1), pairs("dom", 1)]
    routes = [routes[i] for i in ORDER]
    block = jax.ShapeDtypeStruct((count, width), F32)

    def swap(messages):
        return [lax.ppermute(m, ALL, route) for m, route in zip(messages, routes, strict=True)]

    matrix = width * width
    *messages, off = call(
        first_kernel,
        [HBM] * 3,
        [pltpu.VMEM((count, width), F32)] * 4 + [pltpu.VMEM(jac_off.shape, BF16)],
        "first",
        16 * matrix,
        16 * matrix,
        [
            pltpu.VMEM(neighbours.shape, jnp.int32),
            pltpu.VMEM((count, width), F32),
            pltpu.VMEM((4, count, count, width), BF16),
            pltpu.VMEM((4, count, width), F32),
            pltpu.SemaphoreType.DMA((7,)),
        ],
        52,
    )(neighbours, adjoint_start, jac_off)
    came = swap(messages)
    local_call = call(local_kernel, [VMEM] * 4, [block], "local", 8 * matrix, 8 * matrix)
    (local,) = local_call(neighbours, adjoint_start, off, jac_diag)
    adjoint, *messages = call(
        middle_kernel, [VMEM] * 10, [block] * 5, "middle", 20 * matrix, 20 * matrix
    )(neighbours, adjoint_start, source, local, *came, precond, off)
    came = swap(messages)
    (local,) = local_call(neighbours, adjoint, off, jac_diag)

    plane = math.prod(CUT[axis] for axis in FIRST)
    line = math.prod(CUT[axis] for axis in SECOND)
    adjoint, payload = call(
        last_kernel,
        [VMEM] * 10,
        [pltpu.VMEM((count, width), F32), pltpu.VMEM((plane, 8, LANES), F32)],
        "last",
        6 * matrix,
        6 * matrix,
    )(owner.reshape(1, count), adjoint, source, local, *came, precond, surf_map)
    got = lax.all_to_all(payload, FIRST, 0, 0, tiled=True)
    (sums,) = call(
        spread_kernel, [VMEM], [jax.ShapeDtypeStruct((line, 8, LANES), F32)], "spread"
    )(got)
    parts = lax.all_to_all(sums, SECOND, 0, 0, tiled=True)
    adjoint, sensitivity = call(
        finish_kernel,
        [VMEM] * 3,
        [jax.ShapeDtypeStruct((count, width), F32), jax.ShapeDtypeStruct((1, width), F32)],
        "finish",
    )(surface_grad, parts, adjoint)
    return (adjoint, sensitivity)


def solution(mesh):
    cut = Mesh(mesh.devices.reshape(tuple(CUT.values())), ALL)
    return jax.shard_map(
        on_device,
        mesh=cut,
        in_specs=(
            P(ALL, None),
            P(ALL, None),
            P(ALL, None, None, None),
            P(ALL, None, None),
            P(ALL, None, None),
            P(),
            P(ALL, None),
            P(ALL),
            P(ALL, None),
        ),
        out_specs=(P(ALL, None), P(ALL, None)),
        check_vma=False,
    )
```

```python
import math

import jax
import jax.numpy as jnp
from jax import lax
from jax.experimental import pallas as pl
from jax.experimental.pallas import tpu as pltpu
from jax.sharding import Mesh, PartitionSpec as P

CUT = {"z": 8, "y": 4, "core": 2, "x": 4}
ALL = tuple(CUT)
LANES = 128
FIRST, SECOND = (('core', 'z'), ('y', 'x'))
ORDERS = ((3, 2, 1, 0), (3, 1, 2, 0))
F32 = jnp.float32
BF16 = jnp.bfloat16
VMEM = pl.BlockSpec(memory_space=pltpu.VMEM)
HBM = pl.BlockSpec(memory_space=pltpu.HBM)


def pairs(axis, first):
    subs = CUT["x"]
    devices = CUT["z"] * CUT["y"] * CUT["core"] * subs
    route = []
    for device in range(devices):
        dom, sub = divmod(device, subs)
        if axis == "dom":
            doms = devices // subs
            dom = (((dom - first) % doms ^ 1) + first) % doms
        else:
            sub = (((sub - first) % subs ^ 1) + first) % subs
        route.append((device, dom * subs + sub))
    return route


def placed(row, count, target):
    rows = lax.broadcasted_iota(jnp.int32, (count, row.shape[1]), 0)
    return jnp.where(rows == target, row, 0.0).astype(BF16)


def matmul(left, right):
    return jnp.dot(left, right, preferred_element_type=F32)


def message_slots(sweep):
    core, odd = lax.axis_index("core"), lax.axis_index("x") % 2
    four = (1, 2, core), (3, 4, odd), (4, 3, odd), (2, 1, core)
    return [four[i] for i in ORDERS[sweep]]


def step(adjoint, source, local, came, precond_ref):
    residual = source - local
    for part in came:
        residual = residual - part[...]
    count = adjoint.shape[0]
    for row in range(count):
        left = placed(residual[row : row + 1, :], count, row)
        adjoint = adjoint + matmul(left, precond_ref[row])
    return adjoint


def send_all(values, names, off, outs):
    count = values.shape[0]
    for (even, odd, which), out, blocks in zip(message_slots(1), outs, off, strict=True):
        total = jnp.zeros(out.shape, F32)
        for row in range(count):
            here = slice(row, row + 1)
            name = jnp.where(which == 0, names[here, even : even + 1], names[here, odd : odd + 1])
            left = placed(values[here, :], count, name % count)
            total = total + matmul(left, blocks(row))
        out[...] = total


def first_kernel(names_in, adjoint_in, off_in, c0, c1, c2, c3, off, names, adjoint, left, sums, sems):
    slots = [jnp.where(which == 0, even, odd) for even, odd, which in message_slots(0)]
    count = adjoint.shape[0]
    heads = [
        pltpu.make_async_copy(names_in, names, sems.at[5]),
        pltpu.make_async_copy(adjoint_in, adjoint, sems.at[6]),
    ]

    def block(m):
        slot = sum(jnp.where(m == i, slots[i], 0) for i in range(len(slots)))
        return slot, pltpu.make_async_copy(off_in.at[:, slot], off.at[:, slot], sems.at[m])

    for copy in heads:
        copy.start()

    @pl.loop(0, len(slots) + 1)
    def _(m):
        block(m)[1].start()

    for copy in heads:
        copy.wait()
    for m, (even, odd, which) in enumerate(message_slots(0)):
        for row in range(count):
            here = slice(row, row + 1)
            name = jnp.where(which == 0, names[here, even : even + 1], names[here, odd : odd + 1])
            left[m, row] = placed(adjoint[here, :], count, name % count)

    @pl.loop(0, len(slots))
    def _(m):
        slot, copy = block(m)
        copy.wait()
        sums[m] = jnp.zeros(sums.shape[1:], F32)

        @pl.loop(0, count)
        def _(row):
            sums[m] += matmul(left[m, row], off[row, slot])

    for m, out in enumerate((c0, c1, c2, c3)):
        out[...] = sums[m]
    block(len(slots))[1].wait()


def local_kernel(names, adjoint, off, diag, out):
    count = adjoint.shape[0]
    total = jnp.zeros(out.shape, F32)
    for row in range(count):
        values = adjoint[row : row + 1, :]
        total = total + matmul(placed(values, count, names[row : row + 1, 0:1] % count), off[row, 0])
        total = total + matmul(placed(values, count, row), diag[row])
    out[...] = total


def middle_kernel(names, adjoint, source, local, c0, c1, c2, c3, precond, off, new, *outs):
    values = step(adjoint[...], source[...], local[...], (c0, c1, c2, c3), precond)
    new[...] = values
    slots = [jnp.where(which == 0, even, odd) for even, odd, which in message_slots(1)]
    send_all(values, names, [lambda row, slot=slot: off[row, slot] for slot in slots], outs)


def last_kernel(owner, adjoint, source, local, c0, c1, c2, c3, precond, surf, new, payload):
    values = step(adjoint[...], source[...], local[...], (c0, c1, c2, c3), precond)
    new[...] = values
    count, width = values.shape
    contribution = matmul(values.astype(BF16), surf[...]).astype(BF16).astype(F32)
    tile = [
        contribution[row : row + 1, i * LANES : (i + 1) * LANES]
        for row in range(count)
        for i in range(width // LANES)
    ]
    tile += [
        jnp.broadcast_to(owner[0:1, row : row + 1].astype(F32), (1, LANES)) for row in range(count)
    ]
    tile = jnp.concatenate(tile, axis=0)
    for i in range(payload.shape[0]):
        payload[i] = tile


def stride(axis):
    step = 1
    for name in reversed(ALL):
        if name == axis:
            return step
        step *= CUT[name]
    raise ValueError(axis)


def spread_kernel(got, out):
    peers = got.shape[0]
    lanes = (got.shape[1] - 2) // 2
    lane = lax.broadcasted_iota(jnp.int32, (peers, LANES), 1)
    patch = sum(lax.axis_index(axis) * stride(axis) for axis in FIRST)
    place = lane
    for axis in reversed(SECOND):
        patch = patch + place % CUT[axis] * stride(axis)
        place = place // CUT[axis]
    group = out.shape[0]
    patch = jnp.where(lane < group, patch, -1).astype(F32)
    hot = jnp.concatenate(
        [jnp.where(got[:, 2 * lanes + row, :] == patch, 1.0, 0.0).astype(BF16) for row in range(2)],
        axis=0,
    )
    for i in range(lanes):
        rows = jnp.concatenate([got[:, i, :], got[:, lanes + i, :]], axis=0).astype(BF16)
        sums = lax.dot_general(hot, rows, (((0,), (0,)), ((), ())), preferred_element_type=F32)
        out[:, i, :] = sums[:group]
    for i in range(lanes, out.shape[1]):
        out[:, i, :] = jnp.zeros((group, LANES), F32)


def finish_kernel(grad, parts, values, adjoint, out):
    adjoint[...] = values[...]
    total = jnp.sum(parts[...], axis=0)
    for i in range(grad.shape[1] // LANES):
        where = slice(i * LANES, (i + 1) * LANES)
        out[:, where] = grad[:, where] - total[i : i + 1, :]


def call(kernel, specs, outs, name, flops=0, nbytes=0, scratch=(), vmem=8):
    return pl.pallas_call(
        kernel,
        in_specs=specs,
        out_specs=[VMEM] * len(outs),
        out_shape=outs,
        scratch_shapes=scratch,
        name=name,
        compiler_params=pltpu.CompilerParams(vmem_limit_bytes=vmem << 20),
        cost_estimate=pl.CostEstimate(flops=flops, bytes_accessed=nbytes, transcendentals=0),
    )


def on_device(
    adjoint_start, source, jac_off, jac_diag, precond, surf_map, neighbours, owner, surface_grad
):
    count, width = adjoint_start.shape
    routes = [pairs("dom", 0), pairs("sub", 0), pairs("sub", 1), pairs("dom", 1)]
    block = jax.ShapeDtypeStruct((count, width), F32)

    def swap(messages, sweep):
        order = [routes[i] for i in ORDERS[sweep]]
        return [lax.ppermute(m, ALL, route) for m, route in zip(messages, order, strict=True)]

    matrix = width * width
    *messages, off = call(
        first_kernel,
        [HBM] * 3,
        [pltpu.VMEM((count, width), F32)] * 4 + [pltpu.VMEM(jac_off.shape, BF16)],
        "first",
        16 * matrix,
        16 * matrix,
        [
            pltpu.VMEM(neighbours.shape, jnp.int32),
            pltpu.VMEM((count, width), F32),
            pltpu.VMEM((4, count, count, width), BF16),
            pltpu.VMEM((4, count, width), F32),
            pltpu.SemaphoreType.DMA((7,)),
        ],
        52,
    )(neighbours, adjoint_start, jac_off)
    came = swap(messages, 0)
    local_call = call(local_kernel, [VMEM] * 4, [block], "local", 8 * matrix, 8 * matrix)
    (local,) = local_call(neighbours, adjoint_start, off, jac_diag)
    adjoint, *messages = call(
        middle_kernel, [VMEM] * 10, [block] * 5, "middle", 20 * matrix, 20 * matrix
    )(neighbours, adjoint_start, source, local, *came, precond, off)
    came = swap(messages, 1)
    (local,) = local_call(neighbours, adjoint, off, jac_diag)

    plane = math.prod(CUT[axis] for axis in FIRST)
    line = math.prod(CUT[axis] for axis in SECOND)
    adjoint, payload = call(
        last_kernel,
        [VMEM] * 10,
        [pltpu.VMEM((count, width), F32), pltpu.VMEM((plane, 8, LANES), F32)],
        "last",
        6 * matrix,
        6 * matrix,
    )(owner.reshape(1, count), adjoint, source, local, *came, precond, surf_map)
    got = lax.all_to_all(payload, FIRST, 0, 0, tiled=True)
    (sums,) = call(
        spread_kernel, [VMEM], [jax.ShapeDtypeStruct((line, 8, LANES), F32)], "spread"
    )(got)
    parts = lax.all_to_all(sums, SECOND, 0, 0, tiled=True)
    adjoint, sensitivity = call(
        finish_kernel,
        [VMEM] * 3,
        [jax.ShapeDtypeStruct((count, width), F32), jax.ShapeDtypeStruct((1, width), F32)],
        "finish",
    )(surface_grad, parts, adjoint)
    return (adjoint, sensitivity)


def solution(mesh):
    cut = Mesh(mesh.devices.reshape(tuple(CUT.values())), ALL)
    return jax.shard_map(
        on_device,
        mesh=cut,
        in_specs=(
            P(ALL, None),
            P(ALL, None),
            P(ALL, None, None, None),
            P(ALL, None, None),
            P(ALL, None, None),
            P(),
            P(ALL, None),
            P(ALL),
            P(ALL, None),
        ),
        out_specs=(P(ALL, None), P(ALL, None)),
        check_vma=False,
    )
```

```python
import math

import jax
import jax.numpy as jnp
from jax import lax
from jax.experimental import pallas as pl
from jax.experimental.pallas import tpu as pltpu
from jax.sharding import Mesh, PartitionSpec as P

CUT = {"z": 8, "y": 4, "core": 2, "x": 4}
ALL = tuple(CUT)
LANES = 128
FIRST, SECOND = (('core', 'z'), ('y', 'x'))
ORDERS = ((3, 2, 1, 0), (3, 1, 2, 0))
F32 = jnp.float32
BF16 = jnp.bfloat16
VMEM = pl.BlockSpec(memory_space=pltpu.VMEM)
HBM = pl.BlockSpec(memory_space=pltpu.HBM)


def pairs(axis, first):
    subs = CUT["x"]
    devices = CUT["z"] * CUT["y"] * CUT["core"] * subs
    route = []
    for device in range(devices):
        dom, sub = divmod(device, subs)
        if axis == "dom":
            doms = devices // subs
            dom = (((dom - first) % doms ^ 1) + first) % doms
        else:
            sub = (((sub - first) % subs ^ 1) + first) % subs
        route.append((device, dom * subs + sub))
    return route


def placed(row, count, target):
    rows = lax.broadcasted_iota(jnp.int32, (count, row.shape[1]), 0)
    return jnp.where(rows == target, row, 0.0).astype(BF16)


def matmul(left, right):
    return jnp.dot(left, right, preferred_element_type=F32)


def message_slots(sweep):
    core, odd = lax.axis_index("core"), lax.axis_index("x") % 2
    four = (1, 2, core), (3, 4, odd), (4, 3, odd), (2, 1, core)
    return [four[i] for i in ORDERS[sweep]]


def step(adjoint, source, local, came, precond_ref):
    residual = source - local
    for part in came:
        residual = residual - part[...]
    count = adjoint.shape[0]
    for row in range(count):
        left = placed(residual[row : row + 1, :], count, row)
        adjoint = adjoint + matmul(left, precond_ref[row])
    return adjoint


def send_all(values, names, off, outs):
    count = values.shape[0]
    for (even, odd, which), out, blocks in zip(message_slots(1), outs, off, strict=True):
        total = jnp.zeros(out.shape, F32)
        for row in range(count):
            here = slice(row, row + 1)
            name = jnp.where(which == 0, names[here, even : even + 1], names[here, odd : odd + 1])
            left = placed(values[here, :], count, name % count)
            total = total + matmul(left, blocks(row))
        out[...] = total


def first_kernel(names_in, adjoint_in, off_in, c0, c1, c2, c3, off, names, adjoint, sems):
    slots = [jnp.where(which == 0, even, odd) for even, odd, which in message_slots(0)]
    count = adjoint.shape[0]
    heads = [
        pltpu.make_async_copy(names_in, names, sems.at[5]),
        pltpu.make_async_copy(adjoint_in, adjoint, sems.at[6]),
    ]

    def block(m):
        slot = (slots + [0])[m]
        return slot, pltpu.make_async_copy(off_in.at[:, slot], off.at[:, slot], sems.at[m])

    for copy in heads:
        copy.start()

    for m in range(len(slots) + 1):
        block(m)[1].start()

    for copy in heads:
        copy.wait()
    left = {}
    for m, (even, odd, which) in enumerate(message_slots(0)):
        for row in range(count):
            here = slice(row, row + 1)
            name = jnp.where(which == 0, names[here, even : even + 1], names[here, odd : odd + 1])
            left[m, row] = placed(adjoint[here, :], count, name % count)

    for m, out in enumerate((c0, c1, c2, c3)):
        slot, copy = block(m)
        copy.wait()
        parts = [matmul(left[m, row], off[row, slot]) for row in range(count)]
        out[...] = sum(parts[1:], parts[0])
    block(len(slots))[1].wait()


def local_kernel(names, adjoint, off, diag, out):
    count = adjoint.shape[0]
    total = jnp.zeros(out.shape, F32)
    for row in range(count):
        values = adjoint[row : row + 1, :]
        total = total + matmul(placed(values, count, names[row : row + 1, 0:1] % count), off[row, 0])
        total = total + matmul(placed(values, count, row), diag[row])
    out[...] = total


def middle_kernel(names, adjoint, source, local, c0, c1, c2, c3, precond, off, new, *outs):
    values = step(adjoint[...], source[...], local[...], (c0, c1, c2, c3), precond)
    new[...] = values
    slots = [jnp.where(which == 0, even, odd) for even, odd, which in message_slots(1)]
    send_all(values, names, [lambda row, slot=slot: off[row, slot] for slot in slots], outs)


def last_kernel(owner, adjoint, source, local, c0, c1, c2, c3, precond, surf, new, payload):
    values = step(adjoint[...], source[...], local[...], (c0, c1, c2, c3), precond)
    new[...] = values
    count, width = values.shape
    contribution = matmul(values.astype(BF16), surf[...]).astype(BF16).astype(F32)
    tile = [
        contribution[row : row + 1, i * LANES : (i + 1) * LANES]
        for row in range(count)
        for i in range(width // LANES)
    ]
    tile += [
        jnp.broadcast_to(owner[0:1, row : row + 1].astype(F32), (1, LANES)) for row in range(count)
    ]
    tile = jnp.concatenate(tile, axis=0)
    for i in range(payload.shape[0]):
        payload[i] = tile


def stride(axis):
    step = 1
    for name in reversed(ALL):
        if name == axis:
            return step
        step *= CUT[name]
    raise ValueError(axis)


def spread_kernel(got, out):
    peers = got.shape[0]
    lanes = (got.shape[1] - 2) // 2
    lane = lax.broadcasted_iota(jnp.int32, (peers, LANES), 1)
    patch = sum(lax.axis_index(axis) * stride(axis) for axis in FIRST)
    place = lane
    for axis in reversed(SECOND):
        patch = patch + place % CUT[axis] * stride(axis)
        place = place // CUT[axis]
    group = out.shape[0]
    patch = jnp.where(lane < group, patch, -1).astype(F32)
    hot = jnp.concatenate(
        [jnp.where(got[:, 2 * lanes + row, :] == patch, 1.0, 0.0).astype(BF16) for row in range(2)],
        axis=0,
    )
    for i in range(lanes):
        rows = jnp.concatenate([got[:, i, :], got[:, lanes + i, :]], axis=0).astype(BF16)
        sums = lax.dot_general(hot, rows, (((0,), (0,)), ((), ())), preferred_element_type=F32)
        out[:, i, :] = sums[:group]
    for i in range(lanes, out.shape[1]):
        out[:, i, :] = jnp.zeros((group, LANES), F32)


def finish_kernel(grad, parts, values, adjoint, out):
    adjoint[...] = values[...]
    total = jnp.sum(parts[...], axis=0)
    for i in range(grad.shape[1] // LANES):
        where = slice(i * LANES, (i + 1) * LANES)
        out[:, where] = grad[:, where] - total[i : i + 1, :]


def call(kernel, specs, outs, name, flops=0, nbytes=0, scratch=(), vmem=8):
    return pl.pallas_call(
        kernel,
        in_specs=specs,
        out_specs=[VMEM] * len(outs),
        out_shape=outs,
        scratch_shapes=scratch,
        name=name,
        compiler_params=pltpu.CompilerParams(vmem_limit_bytes=vmem << 20),
        cost_estimate=pl.CostEstimate(flops=flops, bytes_accessed=nbytes, transcendentals=0),
    )


LINE = [(0, 7), (0, 6), (0, 5), (0, 4), (0, 3), (0, 2), (0, 1), (0, 0), (1, 7), (1, 6), (1, 5), (1, 4), (1, 3), (1, 2), (1, 1), (1, 0)]


def lines():
    return [
        [z * stride("z") + core * stride("core") + y * stride("y") + x for core, z in LINE]
        for y in range(CUT["y"])
        for x in range(CUT["x"])
    ]


def on_device(
    adjoint_start, source, jac_off, jac_diag, precond, surf_map, neighbours, owner, surface_grad
):
    count, width = adjoint_start.shape
    routes = [pairs("dom", 0), pairs("sub", 0), pairs("sub", 1), pairs("dom", 1)]
    block = jax.ShapeDtypeStruct((count, width), F32)

    def swap(messages, sweep):
        order = [routes[i] for i in ORDERS[sweep]]
        return [lax.ppermute(m, ALL, route) for m, route in zip(messages, order, strict=True)]

    matrix = width * width
    *messages, off = call(
        first_kernel,
        [HBM] * 3,
        [pltpu.VMEM((count, width), F32)] * 4 + [pltpu.VMEM(jac_off.shape, BF16)],
        "first",
        16 * matrix,
        16 * matrix,
        [
            pltpu.VMEM(neighbours.shape, jnp.int32),
            pltpu.VMEM((count, width), F32),
            pltpu.SemaphoreType.DMA((7,)),
        ],
        60,
    )(neighbours, adjoint_start, jac_off)
    came = swap(messages, 0)
    local_call = call(local_kernel, [VMEM] * 4, [block], "local", 8 * matrix, 8 * matrix)
    (local,) = local_call(neighbours, adjoint_start, off, jac_diag)
    adjoint, *messages = call(
        middle_kernel, [VMEM] * 10, [block] * 5, "middle", 20 * matrix, 20 * matrix
    )(neighbours, adjoint_start, source, local, *came, precond, off)
    came = swap(messages, 1)
    (local,) = local_call(neighbours, adjoint, off, jac_diag)

    plane = math.prod(CUT[axis] for axis in FIRST)
    line = math.prod(CUT[axis] for axis in SECOND)
    adjoint, payload = call(
        last_kernel,
        [VMEM] * 10,
        [pltpu.VMEM((count, width), F32), pltpu.VMEM((plane, 8, LANES), F32)],
        "last",
        6 * matrix,
        6 * matrix,
    )(owner.reshape(1, count), adjoint, source, local, *came, precond, surf_map)
    got = lax.all_to_all(payload, ALL, 0, 0, axis_index_groups=lines(), tiled=True)
    (sums,) = call(
        spread_kernel, [VMEM], [jax.ShapeDtypeStruct((line, 8, LANES), F32)], "spread"
    )(got)
    parts = lax.all_to_all(sums, SECOND, 0, 0, tiled=True)
    adjoint, sensitivity = call(
        finish_kernel,
        [VMEM] * 3,
        [jax.ShapeDtypeStruct((count, width), F32), jax.ShapeDtypeStruct((1, width), F32)],
        "finish",
    )(surface_grad, parts, adjoint)
    return (adjoint, sensitivity)


def solution(mesh):
    cut = Mesh(mesh.devices.reshape(tuple(CUT.values())), ALL)
    return jax.shard_map(
        on_device,
        mesh=cut,
        in_specs=(
            P(ALL, None),
            P(ALL, None),
            P(ALL, None, None, None),
            P(ALL, None, None),
            P(ALL, None, None),
            P(),
            P(ALL, None),
            P(ALL),
            P(ALL, None),
        ),
        out_specs=(P(ALL, None), P(ALL, None)),
        check_vma=False,
    )
```

```python
import math

import jax
import jax.numpy as jnp
from jax import lax
from jax.experimental import pallas as pl
from jax.experimental.pallas import tpu as pltpu
from jax.sharding import Mesh, PartitionSpec as P

CUT = {"z": 8, "y": 4, "core": 2, "x": 4}
ALL = tuple(CUT)
LANES = 128
FIRST, SECOND = (('core', 'z'), ('y', 'x'))
ORDERS = ((3, 2, 1, 0), (3, 1, 2, 0))
F32 = jnp.float32
BF16 = jnp.bfloat16
VMEM = pl.BlockSpec(memory_space=pltpu.VMEM)
HBM = pl.BlockSpec(memory_space=pltpu.HBM)


def pairs(axis, first):
    subs = CUT["x"]
    devices = CUT["z"] * CUT["y"] * CUT["core"] * subs
    route = []
    for device in range(devices):
        dom, sub = divmod(device, subs)
        if axis == "dom":
            doms = devices // subs
            dom = (((dom - first) % doms ^ 1) + first) % doms
        else:
            sub = (((sub - first) % subs ^ 1) + first) % subs
        route.append((device, dom * subs + sub))
    return route


def placed(row, count, target):
    rows = lax.broadcasted_iota(jnp.int32, (count, row.shape[1]), 0)
    return jnp.where(rows == target, row, 0.0).astype(BF16)


def matmul(left, right):
    return jnp.dot(left, right, preferred_element_type=F32)


def message_slots(sweep):
    core, odd = lax.axis_index("core"), lax.axis_index("x") % 2
    four = (1, 2, core), (3, 4, odd), (4, 3, odd), (2, 1, core)
    return [four[i] for i in ORDERS[sweep]]


def step(adjoint, source, local, came, precond_ref):
    residual = source - local
    for part in came:
        residual = residual - part[...]
    count = adjoint.shape[0]
    for row in range(count):
        left = placed(residual[row : row + 1, :], count, row)
        adjoint = adjoint + matmul(left, precond_ref[row])
    return adjoint


def send_all(values, names, off, outs):
    count = values.shape[0]
    for (even, odd, which), out, blocks in zip(message_slots(1), outs, off, strict=True):
        total = jnp.zeros(out.shape, F32)
        for row in range(count):
            here = slice(row, row + 1)
            name = jnp.where(which == 0, names[here, even : even + 1], names[here, odd : odd + 1])
            left = placed(values[here, :], count, name % count)
            total = total + matmul(left, blocks(row))
        out[...] = total


def first_kernel(names_in, adjoint_in, off_in, c0, c1, c2, c3, off, names, adjoint, sems):
    slots = [jnp.where(which == 0, even, odd) for even, odd, which in message_slots(0)]
    count = adjoint.shape[0]
    heads = [
        pltpu.make_async_copy(names_in, names, sems.at[5]),
        pltpu.make_async_copy(adjoint_in, adjoint, sems.at[6]),
    ]

    def block(m):
        slot = (slots + [0])[m]
        return slot, pltpu.make_async_copy(off_in.at[:, slot], off.at[:, slot], sems.at[m])

    for copy in heads:
        copy.start()

    for m in range(len(slots) + 1):
        block(m)[1].start()

    for copy in heads:
        copy.wait()
    left = {}
    for m, (even, odd, which) in enumerate(message_slots(0)):
        for row in range(count):
            here = slice(row, row + 1)
            name = jnp.where(which == 0, names[here, even : even + 1], names[here, odd : odd + 1])
            left[m, row] = placed(adjoint[here, :], count, name % count)

    for m, out in enumerate((c0, c1, c2, c3)):
        slot, copy = block(m)
        copy.wait()
        parts = [matmul(left[m, row], off[row, slot]) for row in range(count)]
        out[...] = sum(parts[1:], parts[0])
    block(len(slots))[1].wait()


def local_kernel(names, adjoint, off, diag, out):
    count = adjoint.shape[0]
    total = jnp.zeros(out.shape, F32)
    for row in range(count):
        values = adjoint[row : row + 1, :]
        total = total + matmul(placed(values, count, names[row : row + 1, 0:1] % count), off[row, 0])
        total = total + matmul(placed(values, count, row), diag[row])
    out[...] = total


def middle_kernel(names, adjoint, source, local, c0, c1, c2, c3, precond, off, new, *outs):
    values = step(adjoint[...], source[...], local[...], (c0, c1, c2, c3), precond)
    new[...] = values
    slots = [jnp.where(which == 0, even, odd) for even, odd, which in message_slots(1)]
    send_all(values, names, [lambda row, slot=slot: off[row, slot] for slot in slots], outs)


def last_kernel(owner, adjoint, source, local, c0, c1, c2, c3, precond, surf, new, payload):
    values = step(adjoint[...], source[...], local[...], (c0, c1, c2, c3), precond)
    new[...] = values
    count, width = values.shape
    contribution = matmul(values.astype(BF16), surf[...]).astype(BF16).astype(F32)
    tile = [
        contribution[row : row + 1, i * LANES : (i + 1) * LANES]
        for row in range(count)
        for i in range(width // LANES)
    ]
    tile += [
        jnp.broadcast_to(owner[0:1, row : row + 1].astype(F32), (1, LANES)) for row in range(count)
    ]
    tile = jnp.concatenate(tile, axis=0)
    for i in range(payload.shape[0]):
        payload[i] = tile


def stride(axis):
    step = 1
    for name in reversed(ALL):
        if name == axis:
            return step
        step *= CUT[name]
    raise ValueError(axis)


def spread_kernel(got, out):
    peers = got.shape[0]
    lanes = (got.shape[1] - 2) // 2
    lane = lax.broadcasted_iota(jnp.int32, (peers, LANES), 1)
    patch = sum(lax.axis_index(axis) * stride(axis) for axis in FIRST)
    group = out.shape[0]
    place = jnp.maximum(group - 1 - lane, 0)
    for axis in reversed(SECOND):
        patch = patch + place % CUT[axis] * stride(axis)
        place = place // CUT[axis]
    patch = jnp.where(lane < group, patch, -1).astype(F32)
    hot = jnp.concatenate(
        [jnp.where(got[:, 2 * lanes + row, :] == patch, 1.0, 0.0).astype(BF16) for row in range(2)],
        axis=0,
    )
    for i in range(lanes):
        rows = jnp.concatenate([got[:, i, :], got[:, lanes + i, :]], axis=0).astype(BF16)
        sums = lax.dot_general(hot, rows, (((0,), (0,)), ((), ())), preferred_element_type=F32)
        out[:, i, :] = sums[:group]
    for i in range(lanes, out.shape[1]):
        out[:, i, :] = jnp.zeros((group, LANES), F32)


def finish_kernel(grad, parts, values, adjoint, out):
    adjoint[...] = values[...]
    total = jnp.sum(parts[...], axis=0)
    for i in range(grad.shape[1] // LANES):
        where = slice(i * LANES, (i + 1) * LANES)
        out[:, where] = grad[:, where] - total[i : i + 1, :]


def call(kernel, specs, outs, name, flops=0, nbytes=0, scratch=(), vmem=8):
    return pl.pallas_call(
        kernel,
        in_specs=specs,
        out_specs=[VMEM] * len(outs),
        out_shape=outs,
        scratch_shapes=scratch,
        name=name,
        compiler_params=pltpu.CompilerParams(vmem_limit_bytes=vmem << 20),
        cost_estimate=pl.CostEstimate(flops=flops, bytes_accessed=nbytes, transcendentals=0),
    )


LINE = [(1, 7), (1, 6), (1, 5), (1, 4), (1, 3), (1, 2), (1, 1), (1, 0), (0, 7), (0, 6), (0, 5), (0, 4), (0, 3), (0, 2), (0, 1), (0, 0)]


def lines():
    return [
        [z * stride("z") + core * stride("core") + y * stride("y") + x for core, z in LINE]
        for y in range(CUT["y"])
        for x in range(CUT["x"])
    ]


def planes():
    return [
        [
            z * stride("z") + core * stride("core") + y * stride("y") + x
            for y in reversed(range(CUT["y"]))
            for x in reversed(range(CUT["x"]))
        ]
        for z in range(CUT["z"])
        for core in range(CUT["core"])
    ]


def on_device(
    adjoint_start, source, jac_off, jac_diag, precond, surf_map, neighbours, owner, surface_grad
):
    count, width = adjoint_start.shape
    routes = [pairs("dom", 0), pairs("sub", 0), pairs("sub", 1), pairs("dom", 1)]
    block = jax.ShapeDtypeStruct((count, width), F32)

    def swap(messages, sweep):
        order = [routes[i] for i in ORDERS[sweep]]
        return [lax.ppermute(m, ALL, route) for m, route in zip(messages, order, strict=True)]

    matrix = width * width
    *messages, off = call(
        first_kernel,
        [HBM] * 3,
        [pltpu.VMEM((count, width), F32)] * 4 + [pltpu.VMEM(jac_off.shape, BF16)],
        "first",
        16 * matrix,
        16 * matrix,
        [
            pltpu.VMEM(neighbours.shape, jnp.int32),
            pltpu.VMEM((count, width), F32),
            pltpu.SemaphoreType.DMA((7,)),
        ],
        60,
    )(neighbours, adjoint_start, jac_off)
    came = swap(messages, 0)
    local_call = call(local_kernel, [VMEM] * 4, [block], "local", 8 * matrix, 8 * matrix)
    (local,) = local_call(neighbours, adjoint_start, off, jac_diag)
    adjoint, *messages = call(
        middle_kernel, [VMEM] * 10, [block] * 5, "middle", 20 * matrix, 20 * matrix
    )(neighbours, adjoint_start, source, local, *came, precond, off)
    came = swap(messages, 1)
    (local,) = local_call(neighbours, adjoint, off, jac_diag)

    plane = math.prod(CUT[axis] for axis in FIRST)
    line = math.prod(CUT[axis] for axis in SECOND)
    adjoint, payload = call(
        last_kernel,
        [VMEM] * 10,
        [pltpu.VMEM((count, width), F32), pltpu.VMEM((plane, 8, LANES), F32)],
        "last",
        6 * matrix,
        6 * matrix,
    )(owner.reshape(1, count), adjoint, source, local, *came, precond, surf_map)
    got = lax.all_to_all(payload, ALL, 0, 0, axis_index_groups=lines(), tiled=True)
    (sums,) = call(
        spread_kernel, [VMEM], [jax.ShapeDtypeStruct((line, 8, LANES), F32)], "spread"
    )(got)
    parts = lax.all_to_all(sums, ALL, 0, 0, axis_index_groups=planes(), tiled=True)
    adjoint, sensitivity = call(
        finish_kernel,
        [VMEM] * 3,
        [jax.ShapeDtypeStruct((count, width), F32), jax.ShapeDtypeStruct((1, width), F32)],
        "finish",
    )(surface_grad, parts, adjoint)
    return (adjoint, sensitivity)


def solution(mesh):
    cut = Mesh(mesh.devices.reshape(tuple(CUT.values())), ALL)
    return jax.shard_map(
        on_device,
        mesh=cut,
        in_specs=(
            P(ALL, None),
            P(ALL, None),
            P(ALL, None, None, None),
            P(ALL, None, None),
            P(ALL, None, None),
            P(),
            P(ALL, None),
            P(ALL),
            P(ALL, None),
        ),
        out_specs=(P(ALL, None), P(ALL, None)),
        check_vma=False,
    )
```

```python
import math

import jax
import jax.numpy as jnp
from jax import lax
from jax.experimental import pallas as pl
from jax.experimental.pallas import tpu as pltpu
from jax.sharding import Mesh, PartitionSpec as P

CUT = {"z": 8, "y": 4, "core": 2, "x": 4}
ALL = tuple(CUT)
LANES = 128
FIRST, SECOND = (('core', 'z'), ('y', 'x'))
ORDERS = ((3, 2, 1, 0), (3, 1, 2, 0))
F32 = jnp.float32
BF16 = jnp.bfloat16
VMEM = pl.BlockSpec(memory_space=pltpu.VMEM)
HBM = pl.BlockSpec(memory_space=pltpu.HBM)


def pairs(axis, first):
    subs = CUT["x"]
    devices = CUT["z"] * CUT["y"] * CUT["core"] * subs
    route = []
    for device in range(devices):
        dom, sub = divmod(device, subs)
        if axis == "dom":
            doms = devices // subs
            dom = (((dom - first) % doms ^ 1) + first) % doms
        else:
            sub = (((sub - first) % subs ^ 1) + first) % subs
        route.append((device, dom * subs + sub))
    return route


def placed(row, count, target):
    rows = lax.broadcasted_iota(jnp.int32, (count, row.shape[1]), 0)
    return jnp.where(rows == target, row, 0.0).astype(BF16)


def matmul(left, right):
    return jnp.dot(left, right, preferred_element_type=F32)


def message_slots(sweep):
    core, odd = lax.axis_index("core"), lax.axis_index("x") % 2
    four = (1, 2, core), (3, 4, odd), (4, 3, odd), (2, 1, core)
    return [four[i] for i in ORDERS[sweep]]


def step(adjoint, source, local, came, precond_ref):
    residual = source - local
    for part in came:
        residual = residual - part[...]
    count = adjoint.shape[0]
    for row in range(count):
        left = placed(residual[row : row + 1, :], count, row)
        adjoint = adjoint + matmul(left, precond_ref[row])
    return adjoint


def send_all(values, names, off, outs):
    count = values.shape[0]
    for (even, odd, which), out, blocks in zip(message_slots(1), outs, off, strict=True):
        total = jnp.zeros(out.shape, F32)
        for row in range(count):
            here = slice(row, row + 1)
            name = jnp.where(which == 0, names[here, even : even + 1], names[here, odd : odd + 1])
            left = placed(values[here, :], count, name % count)
            total = total + matmul(left, blocks(row))
        out[...] = total


def first_kernel(names_in, adjoint_in, off_in, c0, c1, c2, c3, off, names, adjoint, sems):
    slots = [jnp.where(which == 0, even, odd) for even, odd, which in message_slots(0)]
    count = adjoint.shape[0]
    heads = [
        pltpu.make_async_copy(names_in, names, sems.at[5]),
        pltpu.make_async_copy(adjoint_in, adjoint, sems.at[6]),
    ]

    def block(m):
        slot = (slots + [0])[m]
        return slot, pltpu.make_async_copy(off_in.at[:, slot], off.at[:, slot], sems.at[m])

    for copy in heads:
        copy.start()

    for m in range(len(slots) + 1):
        block(m)[1].start()

    for copy in heads:
        copy.wait()
    left = {}
    for m, (even, odd, which) in enumerate(message_slots(0)):
        for row in range(count):
            here = slice(row, row + 1)
            name = jnp.where(which == 0, names[here, even : even + 1], names[here, odd : odd + 1])
            left[m, row] = placed(adjoint[here, :], count, name % count)

    for m, out in enumerate((c0, c1, c2, c3)):
        slot, copy = block(m)
        copy.wait()
        parts = [matmul(left[m, row], off[row, slot]) for row in range(count)]
        out[...] = sum(parts[1:], parts[0])
    block(len(slots))[1].wait()


def local_kernel(names, adjoint, off, diag, out):
    count = adjoint.shape[0]
    total = jnp.zeros(out.shape, F32)
    for row in range(count):
        values = adjoint[row : row + 1, :]
        total = total + matmul(placed(values, count, names[row : row + 1, 0:1] % count), off[row, 0])
        total = total + matmul(placed(values, count, row), diag[row])
    out[...] = total


def middle_kernel(names, adjoint, source, local, c0, c1, c2, c3, precond, off, new, *outs):
    values = step(adjoint[...], source[...], local[...], (c0, c1, c2, c3), precond)
    new[...] = values
    slots = [jnp.where(which == 0, even, odd) for even, odd, which in message_slots(1)]
    send_all(values, names, [lambda row, slot=slot: off[row, slot] for slot in slots], outs)


def last_kernel(owner, adjoint, source, local, c0, c1, c2, c3, precond, surf, new, payload):
    values = step(adjoint[...], source[...], local[...], (c0, c1, c2, c3), precond)
    new[...] = values
    count, width = values.shape
    contribution = matmul(values.astype(BF16), surf[...]).astype(BF16).astype(F32)
    tile = [
        contribution[row : row + 1, i * LANES : (i + 1) * LANES]
        for row in range(count)
        for i in range(width // LANES)
    ]
    tile += [
        jnp.broadcast_to(owner[0:1, row : row + 1].astype(F32), (1, LANES)) for row in range(count)
    ]
    tile = jnp.concatenate(tile, axis=0)
    for i in range(payload.shape[0]):
        payload[i] = tile


def stride(axis):
    step = 1
    for name in reversed(ALL):
        if name == axis:
            return step
        step *= CUT[name]
    raise ValueError(axis)


def spread_kernel(got, out):
    peers = got.shape[0]
    lanes = (got.shape[1] - 2) // 2
    lane = lax.broadcasted_iota(jnp.int32, (peers, LANES), 1)
    patch = sum(lax.axis_index(axis) * stride(axis) for axis in FIRST)
    group = out.shape[0]
    place = jnp.maximum(group - 1 - lane, 0)
    for axis in reversed(SECOND):
        patch = patch + place % CUT[axis] * stride(axis)
        place = place // CUT[axis]
    patch = jnp.where(lane < group, patch, -1).astype(F32)
    hot = jnp.concatenate(
        [jnp.where(got[:, 2 * lanes + row, :] == patch, 1.0, 0.0).astype(BF16) for row in range(2)],
        axis=0,
    )
    for i in range(lanes):
        rows = jnp.concatenate([got[:, i, :], got[:, lanes + i, :]], axis=0).astype(BF16)
        sums = lax.dot_general(hot, rows, (((0,), (0,)), ((), ())), preferred_element_type=F32)
        out[:, i, :] = sums[:group]
    for i in range(lanes, out.shape[1]):
        out[:, i, :] = jnp.zeros((group, LANES), F32)


def finish_kernel(grad, parts, values, adjoint, out):
    adjoint[...] = values[...]
    total = jnp.sum(parts[...], axis=0)
    for i in range(grad.shape[1] // LANES):
        where = slice(i * LANES, (i + 1) * LANES)
        out[:, where] = grad[:, where] - total[i : i + 1, :]


def call(kernel, specs, outs, name, flops=0, nbytes=0, scratch=(), vmem=8):
    return pl.pallas_call(
        kernel,
        in_specs=specs,
        out_specs=[VMEM] * len(outs),
        out_shape=outs,
        scratch_shapes=scratch,
        name=name,
        compiler_params=pltpu.CompilerParams(vmem_limit_bytes=vmem << 20),
        cost_estimate=pl.CostEstimate(flops=flops, bytes_accessed=nbytes, transcendentals=0),
    )


LINE = [(1, 7), (0, 7), (1, 6), (0, 6), (1, 5), (0, 5), (1, 4), (0, 4), (1, 3), (0, 3), (1, 2), (0, 2), (1, 1), (0, 1), (1, 0), (0, 0)]


def lines():
    return [
        [z * stride("z") + core * stride("core") + y * stride("y") + x for core, z in LINE]
        for y in range(CUT["y"])
        for x in range(CUT["x"])
    ]


def planes():
    return [
        [
            z * stride("z") + core * stride("core") + y * stride("y") + x
            for y in reversed(range(CUT["y"]))
            for x in reversed(range(CUT["x"]))
        ]
        for z in range(CUT["z"])
        for core in range(CUT["core"])
    ]


def on_device(
    adjoint_start, source, jac_off, jac_diag, precond, surf_map, neighbours, owner, surface_grad
):
    count, width = adjoint_start.shape
    routes = [pairs("dom", 0), pairs("sub", 0), pairs("sub", 1), pairs("dom", 1)]
    block = jax.ShapeDtypeStruct((count, width), F32)

    def swap(messages, sweep):
        order = [routes[i] for i in ORDERS[sweep]]
        return [lax.ppermute(m, ALL, route) for m, route in zip(messages, order, strict=True)]

    matrix = width * width
    *messages, off = call(
        first_kernel,
        [HBM] * 3,
        [pltpu.VMEM((count, width), F32)] * 4 + [pltpu.VMEM(jac_off.shape, BF16)],
        "first",
        16 * matrix,
        16 * matrix,
        [
            pltpu.VMEM(neighbours.shape, jnp.int32),
            pltpu.VMEM((count, width), F32),
            pltpu.SemaphoreType.DMA((7,)),
        ],
        60,
    )(neighbours, adjoint_start, jac_off)
    came = swap(messages, 0)
    local_call = call(local_kernel, [VMEM] * 4, [block], "local", 8 * matrix, 8 * matrix)
    (local,) = local_call(neighbours, adjoint_start, off, jac_diag)
    adjoint, *messages = call(
        middle_kernel, [VMEM] * 10, [block] * 5, "middle", 20 * matrix, 20 * matrix
    )(neighbours, adjoint_start, source, local, *came, precond, off)
    came = swap(messages, 1)
    (local,) = local_call(neighbours, adjoint, off, jac_diag)

    plane = math.prod(CUT[axis] for axis in FIRST)
    line = math.prod(CUT[axis] for axis in SECOND)
    adjoint, payload = call(
        last_kernel,
        [VMEM] * 10,
        [pltpu.VMEM((count, width), F32), pltpu.VMEM((plane, 8, LANES), F32)],
        "last",
        6 * matrix,
        6 * matrix,
    )(owner.reshape(1, count), adjoint, source, local, *came, precond, surf_map)
    got = lax.all_to_all(payload, ALL, 0, 0, axis_index_groups=lines(), tiled=True)
    (sums,) = call(
        spread_kernel, [VMEM], [jax.ShapeDtypeStruct((line, 4, LANES), F32)], "spread"
    )(got)
    parts = lax.all_to_all(sums, ALL, 0, 0, axis_index_groups=planes(), tiled=True)
    adjoint, sensitivity = call(
        finish_kernel,
        [VMEM] * 3,
        [jax.ShapeDtypeStruct((count, width), F32), jax.ShapeDtypeStruct((1, width), F32)],
        "finish",
    )(surface_grad, parts, adjoint)
    return (adjoint, sensitivity)


def solution(mesh):
    cut = Mesh(mesh.devices.reshape(tuple(CUT.values())), ALL)
    return jax.shard_map(
        on_device,
        mesh=cut,
        in_specs=(
            P(ALL, None),
            P(ALL, None),
            P(ALL, None, None, None),
            P(ALL, None, None),
            P(ALL, None, None),
            P(),
            P(ALL, None),
            P(ALL),
            P(ALL, None),
        ),
        out_specs=(P(ALL, None), P(ALL, None)),
        check_vma=False,
    )
```
